32 devices in a mesh: dp: 16 (over z, x, core), tensor: 2 (over y).
Axes of the slice: x: 2, y: 2, z: 4, core: 2. Of those that a mesh axis runs over, the one named last changes fastest.
Arguments:
- hidden_input_state: bfloat16 [6144, 4608], P('dp', 'tensor'), may hold values from -80 to 80
- norm_gain: float32 [4608], replicated, may hold values from 0.5 to 1.5
- head_weight: bfloat16 [4608, 2048], P(None, 'tensor'), may hold values from -2 to 2
- target_ids: int32 [6144], P('dp'), may hold values from 0 to 2047
Outputs:
- hidden_state_gradient: float32 [6144, 4608], P('dp', 'tensor')
- grad_head: float32 [4608, 2048], P('dp', 'tensor')
- norm_gain_gradient: float32 [4608], P('tensor')
The draws below stay inside these ranges and needn't reach their ends.
All inputs are finite; a program needn't handle non-finite values.
Results may differ from the reference program's by a relative error of at most 0.0039.
Values may be sent and summed in bfloat16 or wider, within the bound.
A program may use at most 192 MiB of HBM per device.

```python
import math
import jax
import jax.numpy as jnp
from jax import lax

D = 4608
VOCAB = 2048
TOKENS = 6144


strength_table = (120.0, 160.0, 200.0, 240.0)


def directions(key):
    return jnp.clip(jax.random.normal(jax.random.fold_in(key, 7), (4, D), jnp.float32), -5.0, 5.0)


def common_row(key):
    return jnp.clip(jax.random.normal(jax.random.fold_in(key, 23), (1, D), jnp.float32), -5.0, 5.0)


def draw_head_weight(key, part):
    base = jnp.clip(jax.random.normal(jax.random.fold_in(key, 11), (D, VOCAB), jnp.float32), -5.0, 5.0)
    position = jnp.arange(VOCAB).astype(jnp.float32) / VOCAB
    spread = jax.random.uniform(jax.random.fold_in(key, 12), (VOCAB,), jnp.float32, 0.0, math.log(3.4))
    scale = 0.1 * jnp.exp(math.log(3.0) * position + spread) / math.sqrt(D)
    drawn = base * scale[None, :]
    unit = directions(key)
    which = jnp.arange(VOCAB) - (VOCAB - 8)
    hot = which >= 0
    clipped = jnp.clip(which, 0, 7)
    group = clipped // 2
    strength = jnp.array(strength_table, jnp.float32)[group] + 2.0 * (clipped % 2).astype(jnp.float32)
    aligned = unit[group].T * (strength / D)[None, :] + 0.05 * drawn
    return jnp.where(hot[None, :], aligned, drawn).astype(jnp.bfloat16)


def draw_hidden_input_state(key, part):
    noise = jnp.clip(jax.random.normal(jax.random.fold_in(key, 21), (TOKENS, D), jnp.float32), -5.0, 5.0)
    common = common_row(key)
    return (noise + 0.7 * common).astype(jnp.bfloat16)


def place_ends(entries, rng, low, top_value):
    index_at = [jax.random.randint(jax.random.fold_in(rng, axis), (), 0, length) for axis, length in enumerate(entries.shape)]
    main_axis = entries.shape.index(max(entries.shape))
    beside = index_at[:main_axis] + [(index_at[main_axis] + 1) % entries.shape[main_axis]] + index_at[main_axis + 1:]
    return entries.at[tuple(index_at)].set(low).at[tuple(beside)].set(top_value)


def setup_inputs(seed: int = 0) -> dict:
    seeds = jax.random.split(jax.random.key(seed), 5)
    hidden_input_state = draw_hidden_input_state(jax.random.fold_in(seeds[4], 71), 0)
    norm_gain = jnp.clip(1.0 + 0.1 * jax.random.normal(seeds[1], (D,), jnp.float32), 0.5, 1.5)
    head_weight = draw_head_weight(jax.random.fold_in(seeds[4], 71), 0)
    target_ids = place_ends(jax.random.randint(seeds[3], (TOKENS,), 0, VOCAB), jax.random.fold_in(seeds[3], 1), 0, VOCAB - 1).astype(jnp.int32)
    return {"hidden_input_state": hidden_input_state, "norm_gain": norm_gain, "head_weight": head_weight, "target_ids": target_ids}


epsilon = 1e-06

def reference(hidden_input_state, norm_gain, head_weight, target_ids):
    token_blocks = 8
    gain_row = norm_gain.astype(jnp.float32)
    blocked = hidden_input_state.reshape(token_blocks, -1, D)
    target_blocks = target_ids.reshape(token_blocks, -1)
    column_ids = lax.broadcasted_iota(jnp.int32, (1, VOCAB), 1)

    def one_block(carry, inputs):
        head_total, gain_total = carry
        block_rows, block_targets = inputs
        values = block_rows.astype(jnp.float32)
        scaled_rows = lax.rsqrt(lax.optimization_barrier(jnp.mean(values * values, axis=1, keepdims=True)) + epsilon)
        normalized = values * scaled_rows
        normed = (normalized * gain_row[None, :]).astype(jnp.bfloat16)
        logits = jnp.dot(normed, head_weight, preferred_element_type=jnp.float32)
        row_top = lax.optimization_barrier(jnp.max(logits, axis=1, keepdims=True))
        log_total = row_top + jnp.log(lax.optimization_barrier(jnp.sum(jnp.exp(logits - row_top), axis=1, keepdims=True)))
        onehot = (column_ids == block_targets.astype(jnp.int32)[:, None]).astype(jnp.float32)
        dlogits = (jnp.exp(logits - log_total) - onehot).astype(jnp.bfloat16)
        normed_gradient = lax.dot_general(dlogits, head_weight, (((1,), (1,)), ((), ())), preferred_element_type=jnp.float32)
        weighted_rows = normed_gradient * gain_row[None, :]
        row_inner_sum = lax.optimization_barrier(jnp.mean(weighted_rows * normalized, axis=1, keepdims=True))
        grad_rows = scaled_rows * (weighted_rows - normalized * row_inner_sum)
        head_total = head_total + lax.dot_general(normed, dlogits, (((0,), (0,)), ((), ())), preferred_element_type=jnp.float32)
        gain_total = gain_total + lax.optimization_barrier(jnp.sum(normed_gradient * normalized, axis=0))
        return ((head_total, gain_total), grad_rows)
    start_carry = (jnp.zeros((D, VOCAB), jnp.float32), jnp.zeros((D,), jnp.float32))
    (grad_head, norm_gain_gradient), grad_blocks = lax.scan(one_block, start_carry, (blocked, target_blocks))
    return (grad_blocks.reshape(TOKENS, D), grad_head, norm_gain_gradient)
```

```python
import jax
import jax.numpy as jnp
from jax import lax
from jax.sharding import PartitionSpec as P

epsilon = 1e-06
bf16 = jnp.bfloat16
f32 = jnp.float32


def make(mesh):
    nt = mesh.shape["tensor"]
    ndp = mesh.shape["dp"]
    nc = 2
    nb = 2
    na = ndp // (nc * nb)

    def shift_tensor(x, k):
        return lax.ppermute(x, "tensor", [(i, (i + k) % nt) for i in range(nt)])

    def dp_shift(x, da, db, dc):
        pairs = []
        for a in range(na):
            for b in range(nb):
                for c in range(nc):
                    src = (a * nb + b) * nc + c
                    dst = (((a + da) % na) * nb + (b + db) % nb) * nc + (c + dc) % nc
                    pairs.append((src, dst))
        return lax.ppermute(x, "dp", pairs)

    def shards(h, gain, head, targets):
        rows, cols = h.shape
        width, vocab = head.shape
        t = lax.axis_index("tensor")
        d = lax.axis_index("dp")
        a, b, c = d // (nb * nc), (d // nc) % nb, d % nc

        own_sq = jnp.sum(jnp.square(h.astype(f32)), axis=1)
        sq = own_sq
        for k in range(1, nt):
            sq = sq + shift_tensor(own_sq, k)
        nchunk = 3 if rows % 3 == 0 else 1
        step = rows // nchunk
        got = [[] for _ in range(nt)]
        for i in range(nchunk):
            piece = h[i * step:(i + 1) * step]
            got[0].append(piece)
            for k in range(1, nt):
                got[k].append(shift_tensor(piece, k))
        scaled = lax.rsqrt(sq / width + epsilon)

        def w_block(k):
            return lax.dynamic_slice_in_dim(head, ((t + k) % nt) * cols, cols, axis=0)

        def gain_block(k):
            return lax.dynamic_slice_in_dim(gain, ((t + k) % nt) * cols, cols)

        logit_parts = []
        normed_parts = []
        for i in range(nchunk):
            s = scaled[i * step:(i + 1) * step, None]
            full = jnp.zeros((step, width), bf16)
            for k in range(nt):
                g = gain_block(-k)[None, :]
                n = (got[k][i].astype(f32) * s * g).astype(bf16)
                full = lax.dynamic_update_slice_in_dim(full, n, ((t - k) % nt) * cols, axis=1)
            normed_parts.append(full)
            logit_parts.append(jnp.dot(full, head, preferred_element_type=f32))
        normed = jnp.concatenate(normed_parts, axis=0)
        logits = jnp.concatenate(logit_parts, axis=0)

        top = jnp.max(logits, axis=1)
        total = jnp.sum(jnp.exp(logits - top[:, None]), axis=1)
        stats = jnp.stack([top, total])
        all_stats = [stats] + [shift_tensor(stats, k) for k in range(1, nt)]
        row_top = top
        for s in all_stats[1:]:
            row_top = jnp.maximum(row_top, s[0])
        row_total = sum(s[1] * jnp.exp(s[0] - row_top) for s in all_stats)
        log_total = row_top + jnp.log(row_total)
        ids = t * vocab + lax.broadcasted_iota(jnp.int32, (1, vocab), 1)
        onehot = (ids == targets[:, None]).astype(f32)
        exact = jnp.exp(logits - log_total[:, None]) - onehot
        dlogits = exact.astype(bf16)
        dot_own = jnp.sum(dlogits.astype(f32) * logits, axis=1)
        dot_all = dot_own
        for k in range(1, nt):
            dot_all = dot_all + shift_tensor(dot_own, k)
        row_dot = dot_all / width

        arrived = []
        for k in range(1, nt):
            part = lax.dot_general(dlogits, w_block(k), (((1,), (1,)), ((), ())),
                                   preferred_element_type=f32).astype(bf16)
            arrived.append(shift_tensor(part, k))

        block = width // na
        small = width // ndp
        order = list(range(na // 2, 0, -1)) + list(range(na // 2 + 1, na)) + [0]
        pieces = []
        for k in order:
            to = (a + k) % na
            cut = lax.dynamic_slice_in_dim(normed, to * block, block, axis=1)
            prod = lax.dot_general(cut, dlogits, (((0,), (0,)), ((), ())),
                                   preferred_element_type=f32)
            prod = prod.reshape(nb, nc, small, vocab)
            keep = lax.dynamic_index_in_dim(prod, c, axis=1, keepdims=False)
            away = lax.dynamic_index_in_dim(prod, 1 - c, axis=1, keepdims=False).astype(bf16)
            keep = keep + dp_shift(away, 0, 0, 1).astype(f32)
            mine = lax.dynamic_index_in_dim(keep, b, axis=0, keepdims=False)
            other = lax.dynamic_index_in_dim(keep, 1 - b, axis=0, keepdims=False).astype(bf16)
            mine = mine + dp_shift(other, 0, 1, 0).astype(f32)
            if k:
                mine = dp_shift(mine.astype(bf16), k, 0, 0).astype(f32)
            pieces.append(mine)

        grad = lax.dot_general(dlogits, w_block(0), (((1,), (1,)), ((), ())),
                               preferred_element_type=f32)
        for p in arrived:
            grad = grad + p.astype(f32)
        normalized = h.astype(f32) * scaled[:, None]
        hidden = scaled[:, None] * (grad * gain_block(0)[None, :] - normalized * row_dot[:, None])
        gain_grad = jnp.sum(grad * normalized, axis=0)
        gain_grad = gain_grad + dp_shift(gain_grad, 0, 0, 1)
        gain_grad = gain_grad + dp_shift(gain_grad, 0, 1, 0)
        gain_grad = gain_grad + sum(dp_shift(gain_grad, k, 0, 0) for k in range(1, na))
        grad_head = pieces[-1]
        for p in pieces[:-1]:
            grad_head = grad_head + p
        return hidden, grad_head, gain_grad

    return shards


def solution(mesh):
    return jax.shard_map(
        make(mesh),
        mesh=mesh,
        in_specs=(P("dp", "tensor"), P(), P(None, "tensor"), P("dp")),
        out_specs=(P("dp", "tensor"), P("dp", "tensor"), P("tensor")),
        check_vma=False,
    )
```

```python
import jax
import jax.numpy as jnp
from jax import lax
from jax.sharding import PartitionSpec as P

epsilon = 1e-06
bf16 = jnp.bfloat16
f32 = jnp.float32


def after(x, dep):
    return lax.optimization_barrier((x, dep))[0]


def make(mesh):
    nt = mesh.shape["tensor"]
    ndp = mesh.shape["dp"]
    nc = 2
    nb = 2
    na = ndp // (nc * nb)

    def shift_tensor(x, k):
        return lax.ppermute(x, "tensor", [(i, (i + k) % nt) for i in range(nt)])

    def dp_shift(x, da, db, dc):
        pairs = []
        for a in range(na):
            for b in range(nb):
                for c in range(nc):
                    src = (a * nb + b) * nc + c
                    dst = (((a + da) % na) * nb + (b + db) % nb) * nc + (c + dc) % nc
                    pairs.append((src, dst))
        return lax.ppermute(x, "dp", pairs)

    def dp_to(x, move):
        pairs = []
        for i in range(ndp):
            a, rest = i // (nb * nc), i % (nb * nc)
            pairs.append((i, move(a) * nb * nc + rest))
        return lax.ppermute(x, "dp", pairs)

    def shards(h, gain, head, targets):
        rows, cols = h.shape
        width, vocab = head.shape
        t = lax.axis_index("tensor")
        d = lax.axis_index("dp")
        a, b, c = d // (nb * nc), (d // nc) % nb, d % nc

        own_sq = jnp.sum(jnp.square(h.astype(f32)), axis=1)
        sq = own_sq
        for k in range(1, nt):
            sq = sq + shift_tensor(own_sq, k)
        nchunk = 3 if rows % 3 == 0 else 1
        step = rows // nchunk
        got = [[] for _ in range(nt)]
        for i in range(nchunk):
            piece = h[i * step:(i + 1) * step]
            got[0].append(piece)
            for k in range(1, nt):
                got[k].append(shift_tensor(piece, k))
        scaled = lax.rsqrt(sq / width + epsilon)

        def w_block(k):
            return lax.dynamic_slice_in_dim(head, ((t + k) % nt) * cols, cols, axis=0)

        def gain_block(k):
            return lax.dynamic_slice_in_dim(gain, ((t + k) % nt) * cols, cols)

        logit_parts = []
        normed_parts = []
        for i in range(nchunk):
            s = scaled[i * step:(i + 1) * step, None]
            full = jnp.zeros((step, width), bf16)
            for k in range(nt):
                g = gain_block(-k)[None, :]
                n = (got[k][i].astype(f32) * s * g).astype(bf16)
                full = lax.dynamic_update_slice_in_dim(full, n, ((t - k) % nt) * cols, axis=1)
            normed_parts.append(full)
            logit_parts.append(jnp.dot(full, head, preferred_element_type=f32))
        normed = jnp.concatenate(normed_parts, axis=0)
        logits = jnp.concatenate(logit_parts, axis=0)

        top = jnp.max(logits, axis=1)
        total = jnp.sum(jnp.exp(logits - top[:, None]), axis=1)
        stats = jnp.stack([top, total])
        all_stats = [stats] + [shift_tensor(stats, k) for k in range(1, nt)]
        row_top = top
        for s in all_stats[1:]:
            row_top = jnp.maximum(row_top, s[0])
        row_total = sum(s[1] * jnp.exp(s[0] - row_top) for s in all_stats)
        log_total = row_top + jnp.log(row_total)
        ids = t * vocab + lax.broadcasted_iota(jnp.int32, (1, vocab), 1)
        onehot = (ids == targets[:, None]).astype(f32)
        exact = jnp.exp(logits - log_total[:, None]) - onehot
        dlogits = exact.astype(bf16)
        dot_own = jnp.sum(dlogits.astype(f32) * logits, axis=1)
        arrived = []
        for k in range(1, nt):
            part = lax.dot_general(dlogits, w_block(k), (((1,), (1,)), ((), ())),
                                   preferred_element_type=f32).astype(bf16)
            arrived.append(shift_tensor(part, k))

        block = width // na
        small = width // ndp
        def halves(to):
            cut = lax.dynamic_slice_in_dim(normed, to * block, block, axis=1)
            prod = lax.dot_general(cut, dlogits, (((0,), (0,)), ((), ())),
                                   preferred_element_type=f32)
            prod = prod.reshape(nb, nc, small, vocab)
            keep = lax.dynamic_index_in_dim(prod, c, axis=1, keepdims=False)
            away = lax.dynamic_index_in_dim(prod, 1 - c, axis=1, keepdims=False).astype(bf16)
            keep = keep + dp_shift(away, 0, 0, 1).astype(f32)
            mine = lax.dynamic_index_in_dim(keep, b, axis=0, keepdims=False)
            other = lax.dynamic_index_in_dim(keep, 1 - b, axis=0, keepdims=False).astype(bf16)
            return mine, dp_shift(other, 0, 1, 0)

        def partial(to):
            mine, other = halves(to)
            return mine + other.astype(f32)

        if na == 4:
            near = a + 1 - 2 * (a % 2)
            first = partial(na - 1 - near).astype(bf16)
            first_in = dp_to(first, lambda i: i ^ 1)
            mine, other = halves(na - 1 - a)
            other = after(other, first)
            second = (mine + other.astype(f32) + first_in.astype(f32)).astype(bf16)
            second_in = dp_to(second, lambda i: na - 1 - i)
            arrived = [after(p, second) for p in arrived]
            mine, other = halves(near)
            other = after(other, second)
            third = (mine + other.astype(f32)).astype(bf16)
            third_in = dp_to(third, lambda i: i ^ 1)
            mine, other = halves(a)
            other = after(other, third)
            grad_head = (mine + other.astype(f32) + third_in.astype(f32)
                         + second_in.astype(f32))
        else:
            grad_head = 0.0
            for k in list(range(na // 2, 0, -1)) + list(range(na // 2 + 1, na)):
                got_block = dp_shift(partial((a + k) % na).astype(bf16), k, 0, 0)
                grad_head = grad_head + got_block.astype(f32)
            grad_head = grad_head + partial(a)

        if arrived:
            dot_own = after(dot_own, arrived)
        dot_all = dot_own
        for k in range(1, nt):
            dot_all = dot_all + shift_tensor(dot_own, k)
        row_dot = dot_all / width

        grad = lax.dot_general(dlogits, w_block(0), (((1,), (1,)), ((), ())),
                               preferred_element_type=f32)
        for p in arrived:
            grad = grad + p.astype(f32)
        normalized = h.astype(f32) * scaled[:, None]
        hidden = scaled[:, None] * (grad * gain_block(0)[None, :] - normalized * row_dot[:, None])
        gain_grad = jnp.sum(grad * normalized, axis=0)
        gain_grad = gain_grad + dp_shift(gain_grad, 0, 0, 1)
        gain_grad = gain_grad + dp_shift(gain_grad, 0, 1, 0)
        gain_grad = gain_grad + sum(dp_shift(gain_grad, k, 0, 0) for k in range(1, na))
        return hidden, grad_head, gain_grad

    return shards


def solution(mesh):
    return jax.shard_map(
        make(mesh),
        mesh=mesh,
        in_specs=(P("dp", "tensor"), P(), P(None, "tensor"), P("dp")),
        out_specs=(P("dp", "tensor"), P("dp", "tensor"), P("tensor")),
        check_vma=False,
    )
```

```python
import jax
import jax.numpy as jnp
from jax import lax
from jax.sharding import PartitionSpec as P

epsilon = 1e-06
bf16 = jnp.bfloat16
f32 = jnp.float32


def after(x, dep):
    return lax.optimization_barrier((x, dep))[0]


def make(mesh):
    nt = mesh.shape["tensor"]
    ndp = mesh.shape["dp"]
    nc = 2
    nb = 2
    na = ndp // (nc * nb)

    def shift_tensor(x, k):
        return lax.ppermute(x, "tensor", [(i, (i + k) % nt) for i in range(nt)])

    def dp_shift(x, da, db, dc):
        pairs = []
        for a in range(na):
            for b in range(nb):
                for c in range(nc):
                    src = (a * nb + b) * nc + c
                    dst = (((a + da) % na) * nb + (b + db) % nb) * nc + (c + dc) % nc
                    pairs.append((src, dst))
        return lax.ppermute(x, "dp", pairs)

    def dp_to(x, move):
        pairs = []
        for i in range(ndp):
            a, rest = i // (nb * nc), i % (nb * nc)
            pairs.append((i, move(a) * nb * nc + rest))
        return lax.ppermute(x, "dp", pairs)

    def shards(h, gain, head, targets):
        rows, cols = h.shape
        width, vocab = head.shape
        t = lax.axis_index("tensor")
        d = lax.axis_index("dp")
        a, b, c = d // (nb * nc), (d // nc) % nb, d % nc

        nchunk = 3 if rows % 3 == 0 else 1
        step = rows // nchunk
        got = [[h[i * step:(i + 1) * step] for i in range(nchunk)]] + [[] for _ in range(1, nt)]
        lead = lax.optimization_barrier(got[0][0])
        own_sq = jnp.sum(jnp.square(after(h, lead).astype(f32)), axis=1)
        for i in range(nchunk):
            piece = lead if i == 0 else after(got[0][i], own_sq)
            for k in range(1, nt):
                got[k].append(shift_tensor(piece, k))
        sq = own_sq
        for k in range(1, nt):
            sq = sq + shift_tensor(own_sq, k)
        scaled = lax.rsqrt(sq / width + epsilon)

        def w_block(k):
            return lax.dynamic_slice_in_dim(head, ((t + k) % nt) * cols, cols, axis=0)

        def gain_block(k):
            return lax.dynamic_slice_in_dim(gain, ((t + k) % nt) * cols, cols)

        logit_parts = []
        normed_parts = []
        for i in range(nchunk):
            s = scaled[i * step:(i + 1) * step, None]
            full = jnp.zeros((step, width), bf16)
            for k in range(nt):
                g = gain_block(-k)[None, :]
                n = (got[k][i].astype(f32) * s * g).astype(bf16)
                full = lax.dynamic_update_slice_in_dim(full, n, ((t - k) % nt) * cols, axis=1)
            normed_parts.append(full)
            logit_parts.append(jnp.dot(full, head, preferred_element_type=f32))
        normed = jnp.concatenate(normed_parts, axis=0)
        logits = jnp.concatenate(logit_parts, axis=0)

        top = jnp.max(logits, axis=1)
        total = jnp.sum(jnp.exp(logits - top[:, None]), axis=1)
        stats = jnp.stack([top, total])
        all_stats = [stats] + [shift_tensor(stats, k) for k in range(1, nt)]
        row_top = top
        for s in all_stats[1:]:
            row_top = jnp.maximum(row_top, s[0])
        row_total = sum(s[1] * jnp.exp(s[0] - row_top) for s in all_stats)
        log_total = row_top + jnp.log(row_total)
        ids = t * vocab + lax.broadcasted_iota(jnp.int32, (1, vocab), 1)
        onehot = (ids == targets[:, None]).astype(f32)
        exact = jnp.exp(logits - log_total[:, None]) - onehot
        dlogits = exact.astype(bf16)
        dot_own = jnp.sum(dlogits.astype(f32) * logits, axis=1)
        arrived = []
        for k in range(1, nt):
            part = lax.dot_general(dlogits, w_block(k), (((1,), (1,)), ((), ())),
                                   preferred_element_type=f32).astype(bf16)
            arrived.append(shift_tensor(part, k))

        block = width // na
        small = width // ndp
        head_grad = dlogits

        def halves(to):
            cut = lax.dynamic_slice_in_dim(normed, to * block, block, axis=1)
            prod = lax.dot_general(cut, head_grad, (((0,), (0,)), ((), ())),
                                   preferred_element_type=f32)
            prod = prod.reshape(nb, nc, small, vocab)
            keep = lax.dynamic_index_in_dim(prod, c, axis=1, keepdims=False)
            away = lax.dynamic_index_in_dim(prod, 1 - c, axis=1, keepdims=False).astype(bf16)
            keep = keep + dp_shift(away, 0, 0, 1).astype(f32)
            mine = lax.dynamic_index_in_dim(keep, b, axis=0, keepdims=False)
            other = lax.dynamic_index_in_dim(keep, 1 - b, axis=0, keepdims=False).astype(bf16)
            return mine, dp_shift(other, 0, 1, 0)

        def partial(to):
            mine, other = halves(to)
            return mine + other.astype(f32)

        if na == 4:
            near = a + 1 - 2 * (a % 2)
            first = partial(na - 1 - near).astype(bf16)
            first_in = dp_to(first, lambda i: i ^ 1)
            mine, other = halves(na - 1 - a)
            other = after(other, first)
            second = (mine + other.astype(f32) + first_in.astype(f32)).astype(bf16)
            second_in = dp_to(second, lambda i: na - 1 - i)
            arrived = [after(p, second) for p in arrived]
            mine, other = halves(near)
            other = after(other, second)
            third = (mine + other.astype(f32)).astype(bf16)
            third_in = dp_to(third, lambda i: i ^ 1)
            mine, other = halves(a)
            other = after(other, third)
            grad_head = (mine + other.astype(f32) + third_in.astype(f32)
                         + second_in.astype(f32))
        else:
            grad_head = 0.0
            for k in list(range(na // 2, 0, -1)) + list(range(na // 2 + 1, na)):
                got_block = dp_shift(partial((a + k) % na).astype(bf16), k, 0, 0)
                grad_head = grad_head + got_block.astype(f32)
            grad_head = grad_head + partial(a)

        if arrived:
            dot_own = after(dot_own, arrived)
        dot_all = dot_own
        for k in range(1, nt):
            dot_all = dot_all + shift_tensor(dot_own, k)
        row_dot = dot_all / width

        grad = lax.dot_general(dlogits, w_block(0), (((1,), (1,)), ((), ())),
                               preferred_element_type=f32)
        for p in arrived:
            grad = grad + p.astype(f32)
        normalized = h.astype(f32) * scaled[:, None]
        hidden = scaled[:, None] * (grad * gain_block(0)[None, :] - normalized * row_dot[:, None])
        gain_grad = jnp.sum(grad * normalized, axis=0)
        gain_grad = gain_grad + dp_shift(gain_grad, 0, 0, 1)
        gain_grad = gain_grad + dp_shift(gain_grad, 0, 1, 0)
        gain_grad = gain_grad + sum(dp_shift(gain_grad, k, 0, 0) for k in range(1, na))
        return hidden, grad_head, gain_grad

    return shards


def solution(mesh):
    return jax.shard_map(
        make(mesh),
        mesh=mesh,
        in_specs=(P("dp", "tensor"), P(), P(None, "tensor"), P("dp")),
        out_specs=(P("dp", "tensor"), P("dp", "tensor"), P("tensor")),
        check_vma=False,
    )
```

```python
import jax
import jax.numpy as jnp
from jax import lax
from jax.sharding import PartitionSpec as P

epsilon = 1e-06
bf16 = jnp.bfloat16
f32 = jnp.float32


def after(x, dep):
    return lax.optimization_barrier((x, dep))[0]


def make(mesh):
    nt = mesh.shape["tensor"]
    ndp = mesh.shape["dp"]
    nc = 2
    nb = 2
    na = ndp // (nc * nb)

    def shift_tensor(x, k):
        return lax.ppermute(x, "tensor", [(i, (i + k) % nt) for i in range(nt)])

    def dp_shift(x, da, db, dc):
        pairs = []
        for a in range(na):
            for b in range(nb):
                for c in range(nc):
                    src = (a * nb + b) * nc + c
                    dst = (((a + da) % na) * nb + (b + db) % nb) * nc + (c + dc) % nc
                    pairs.append((src, dst))
        return lax.ppermute(x, "dp", pairs)

    def dp_to(x, move):
        pairs = []
        for i in range(ndp):
            a, rest = i // (nb * nc), i % (nb * nc)
            pairs.append((i, move(a) * nb * nc + rest))
        return lax.ppermute(x, "dp", pairs)

    def shards(h, gain, head, targets):
        rows, cols = h.shape
        width, vocab = head.shape
        t = lax.axis_index("tensor")
        d = lax.axis_index("dp")
        a, b, c = d // (nb * nc), (d // nc) % nb, d % nc

        nchunk = 3 if rows % 3 == 0 else 1
        step = rows // nchunk
        got = [[h[i * step:(i + 1) * step] for i in range(nchunk)]] + [[] for _ in range(1, nt)]
        pieces = lax.optimization_barrier(got[0])
        for piece in pieces:
            for k in range(1, nt):
                got[k].append(shift_tensor(piece, k))

        def w_block(k):
            return lax.dynamic_slice_in_dim(head, ((t + k) % nt) * cols, cols, axis=0)

        def gain_block(k):
            return lax.dynamic_slice_in_dim(gain, ((t + k) % nt) * cols, cols)

        logit_parts = []
        normed_parts = []
        scaled_parts = []
        for i in range(nchunk):
            parts = [got[k][i] for k in range(nt)]
            if i:
                parts = [parts[0]] + [after(p, logit_parts[-1]) for p in parts[1:]]
            sq = sum(jnp.sum(jnp.square(p.astype(f32)), axis=1) for p in parts)
            scaled = lax.rsqrt(sq / width + epsilon)
            full = jnp.zeros((step, width), bf16)
            for k in range(nt):
                g = gain_block(-k)[None, :]
                n = (parts[k].astype(f32) * scaled[:, None] * g).astype(bf16)
                full = lax.dynamic_update_slice_in_dim(full, n, ((t - k) % nt) * cols, axis=1)
            normed_parts.append(full)
            scaled_parts.append(scaled)
            logit_parts.append(jnp.dot(full, head, preferred_element_type=f32))
        scaled = jnp.concatenate(scaled_parts)
        normed = jnp.concatenate(normed_parts, axis=0)
        logits = jnp.concatenate(logit_parts, axis=0)

        top = jnp.max(logits, axis=1)
        total = jnp.sum(jnp.exp(logits - top[:, None]), axis=1)
        stats = jnp.stack([top, total])
        all_stats = [stats] + [shift_tensor(stats, k) for k in range(1, nt)]
        row_top = top
        for s in all_stats[1:]:
            row_top = jnp.maximum(row_top, s[0])
        row_total = sum(s[1] * jnp.exp(s[0] - row_top) for s in all_stats)
        log_total = row_top + jnp.log(row_total)
        ids = t * vocab + lax.broadcasted_iota(jnp.int32, (1, vocab), 1)
        onehot = (ids == targets[:, None]).astype(f32)
        exact = jnp.exp(logits - log_total[:, None]) - onehot
        dlogits = exact.astype(bf16)
        dot_own = jnp.sum(dlogits.astype(f32) * logits, axis=1)
        arrived = []
        for k in range(1, nt):
            part = lax.dot_general(dlogits, w_block(k), (((1,), (1,)), ((), ())),
                                   preferred_element_type=f32).astype(bf16)
            arrived.append(shift_tensor(part, k))

        block = width // na
        small = width // ndp
        head_grad = dlogits

        def halves(to):
            cut = lax.dynamic_slice_in_dim(normed, to * block, block, axis=1)
            prod = lax.dot_general(cut, head_grad, (((0,), (0,)), ((), ())),
                                   preferred_element_type=f32)
            prod = prod.reshape(nb, nc, small, vocab)
            keep = lax.dynamic_index_in_dim(prod, c, axis=1, keepdims=False)
            away = lax.dynamic_index_in_dim(prod, 1 - c, axis=1, keepdims=False).astype(bf16)
            keep = keep + dp_shift(away, 0, 0, 1).astype(f32)
            mine = lax.dynamic_index_in_dim(keep, b, axis=0, keepdims=False)
            other = lax.dynamic_index_in_dim(keep, 1 - b, axis=0, keepdims=False).astype(bf16)
            return mine, dp_shift(other, 0, 1, 0)

        def partial(to):
            mine, other = halves(to)
            return mine + other.astype(f32)

        if na == 4:
            near = a + 1 - 2 * (a % 2)
            first = partial(na - 1 - near).astype(bf16)
            first_in = dp_to(first, lambda i: i ^ 1)
            mine, other = halves(na - 1 - a)
            other = after(other, first)
            second = (mine + other.astype(f32) + first_in.astype(f32)).astype(bf16)
            second_in = dp_to(second, lambda i: na - 1 - i)
            arrived = [after(p, second) for p in arrived]
            mine, other = halves(near)
            other = after(other, second)
            third = (mine + other.astype(f32)).astype(bf16)
            third_in = dp_to(third, lambda i: i ^ 1)
            mine, other = halves(a)
            other = after(other, third)
            grad_head = (mine + other.astype(f32) + third_in.astype(f32)
                         + second_in.astype(f32))
        else:
            grad_head = 0.0
            for k in list(range(na // 2, 0, -1)) + list(range(na // 2 + 1, na)):
                got_block = dp_shift(partial((a + k) % na).astype(bf16), k, 0, 0)
                grad_head = grad_head + got_block.astype(f32)
            grad_head = grad_head + partial(a)

        if arrived:
            dot_own = after(dot_own, arrived)
        dot_all = dot_own
        for k in range(1, nt):
            dot_all = dot_all + shift_tensor(dot_own, k)
        row_dot = dot_all / width

        own = lax.dot_general(dlogits, w_block(0), (((1,), (1,)), ((), ())),
                              preferred_element_type=f32)
        normalized = h.astype(f32) * scaled[:, None]

        def total_grad(terms):
            return sum(p.astype(f32) for p in terms)

        gain_grad = jnp.sum(total_grad([own] + arrived) * normalized, axis=0)
        grad = total_grad(after([own] + arrived, gain_grad))
        hidden = scaled[:, None] * (grad * gain_block(0)[None, :] - normalized * row_dot[:, None])
        gain_grad = gain_grad + dp_shift(gain_grad, 0, 0, 1)
        gain_grad = gain_grad + dp_shift(gain_grad, 0, 1, 0)
        gain_grad = gain_grad + sum(dp_shift(gain_grad, k, 0, 0) for k in range(1, na))
        return hidden, grad_head, gain_grad

    return shards


def solution(mesh):
    return jax.shard_map(
        make(mesh),
        mesh=mesh,
        in_specs=(P("dp", "tensor"), P(), P(None, "tensor"), P("dp")),
        out_specs=(P("dp", "tensor"), P("dp", "tensor"), P("tensor")),
        check_vma=False,
    )
```

```python
import jax
import jax.numpy as jnp
from jax import lax
from jax.sharding import PartitionSpec as P

epsilon = 1e-06
bf16 = jnp.bfloat16
f32 = jnp.float32


def after(x, dep):
    return lax.optimization_barrier((x, dep))[0]


def make(mesh):
    nt = mesh.shape["tensor"]
    ndp = mesh.shape["dp"]
    nc = 2
    nb = 2
    na = ndp // (nc * nb)

    def shift_tensor(x, k):
        return lax.ppermute(x, "tensor", [(i, (i + k) % nt) for i in range(nt)])

    def dp_shift(x, da, db, dc):
        pairs = []
        for a in range(na):
            for b in range(nb):
                for c in range(nc):
                    src = (a * nb + b) * nc + c
                    dst = (((a + da) % na) * nb + (b + db) % nb) * nc + (c + dc) % nc
                    pairs.append((src, dst))
        return lax.ppermute(x, "dp", pairs)

    def dp_to(x, move):
        pairs = []
        for i in range(ndp):
            a, rest = i // (nb * nc), i % (nb * nc)
            pairs.append((i, move(a) * nb * nc + rest))
        return lax.ppermute(x, "dp", pairs)

    def shards(h, gain, head, targets):
        rows, cols = h.shape
        width, vocab = head.shape
        t = lax.axis_index("tensor")
        d = lax.axis_index("dp")
        a, b, c = d // (nb * nc), (d // nc) % nb, d % nc

        nchunk = 3 if rows % 3 == 0 else 1
        step = rows // nchunk
        got = [[h[i * step:(i + 1) * step] for i in range(nchunk)]] + [[] for _ in range(1, nt)]
        lead = lax.optimization_barrier(got[0][0])
        own_sq = jnp.sum(jnp.square(after(h, lead).astype(f32)), axis=1)
        for i in range(nchunk):
            piece = lead if i == 0 else after(got[0][i], own_sq)
            for k in range(1, nt):
                got[k].append(shift_tensor(piece, k))
        sq = own_sq
        for k in range(1, nt):
            sq = sq + shift_tensor(own_sq, k)
        scaled = lax.rsqrt(sq / width + epsilon)

        def w_block(k):
            return lax.dynamic_slice_in_dim(head, ((t + k) % nt) * cols, cols, axis=0)

        def gain_block(k):
            return lax.dynamic_slice_in_dim(gain, ((t + k) % nt) * cols, cols)

        logit_parts = []
        normed_parts = []
        for i in range(nchunk):
            s = scaled[i * step:(i + 1) * step, None]
            full = jnp.zeros((step, width), bf16)
            for k in range(nt):
                g = gain_block(-k)[None, :]
                n = (got[k][i].astype(f32) * s * g).astype(bf16)
                full = lax.dynamic_update_slice_in_dim(full, n, ((t - k) % nt) * cols, axis=1)
            normed_parts.append(full)
            logit_parts.append(jnp.dot(full, head, preferred_element_type=f32))
        normed = jnp.concatenate(normed_parts, axis=0)
        logits = jnp.concatenate(logit_parts, axis=0)

        top = jnp.max(logits, axis=1)
        total = jnp.sum(jnp.exp(logits - top[:, None]), axis=1)
        stats = jnp.stack([top, total])
        all_stats = [stats] + [shift_tensor(stats, k) for k in range(1, nt)]
        row_top = top
        for s in all_stats[1:]:
            row_top = jnp.maximum(row_top, s[0])
        row_total = sum(s[1] * jnp.exp(s[0] - row_top) for s in all_stats)
        log_total = row_top + jnp.log(row_total)
        ids = t * vocab + lax.broadcasted_iota(jnp.int32, (1, vocab), 1)
        onehot = (ids == targets[:, None]).astype(f32)
        exact = jnp.exp(logits - log_total[:, None]) - onehot
        dlogits = exact.astype(bf16)
        dot_own = jnp.sum(dlogits.astype(f32) * logits, axis=1)
        arrived = []
        for k in range(1, nt):
            part = lax.dot_general(dlogits, w_block(k), (((1,), (1,)), ((), ())),
                                   preferred_element_type=f32).astype(bf16)
            arrived.append(shift_tensor(part, k))

        block = width // na
        small = width // ndp
        head_grad = dlogits

        def halves(to):
            cut = lax.dynamic_slice_in_dim(normed, to * block, block, axis=1)
            prod = lax.dot_general(cut, head_grad, (((0,), (0,)), ((), ())),
                                   preferred_element_type=f32)
            prod = prod.reshape(nb, nc, small, vocab)
            keep = lax.dynamic_index_in_dim(prod, c, axis=1, keepdims=False)
            away = lax.dynamic_index_in_dim(prod, 1 - c, axis=1, keepdims=False).astype(bf16)
            keep = keep + dp_shift(away, 0, 0, 1).astype(f32)
            mine = lax.dynamic_index_in_dim(keep, b, axis=0, keepdims=False)
            other = lax.dynamic_index_in_dim(keep, 1 - b, axis=0, keepdims=False).astype(bf16)
            return mine, dp_shift(other, 0, 1, 0)

        def partial(to):
            mine, other = halves(to)
            return mine + other.astype(f32)

        if na == 4:
            near = a + 1 - 2 * (a % 2)
            first = partial(na - 1 - near).astype(bf16)
            first_in = dp_to(first, lambda i: i ^ 1)
            mine, other = halves(na - 1 - a)
            other = after(other, first)
            second = (mine + other.astype(f32) + first_in.astype(f32)).astype(bf16)
            second_in = dp_to(second, lambda i: na - 1 - i)
            arrived = [after(p, first) for p in arrived]
            mine, other = halves(near)
            other = after(other, second)
            third = (mine + other.astype(f32)).astype(bf16)
            third_in = dp_to(third, lambda i: i ^ 1)
            mine, other = halves(a)
            other = after(other, third)
            grad_head = (mine + other.astype(f32) + third_in.astype(f32)
                         + second_in.astype(f32))
        else:
            grad_head = 0.0
            for k in list(range(na // 2, 0, -1)) + list(range(na // 2 + 1, na)):
                got_block = dp_shift(partial((a + k) % na).astype(bf16), k, 0, 0)
                grad_head = grad_head + got_block.astype(f32)
            grad_head = grad_head + partial(a)

        if arrived:
            dot_own = after(dot_own, arrived)
        dot_all = dot_own
        for k in range(1, nt):
            dot_all = dot_all + shift_tensor(dot_own, k)
        row_dot = dot_all / width

        grad = lax.dot_general(dlogits, w_block(0), (((1,), (1,)), ((), ())),
                               preferred_element_type=f32)
        for p in arrived:
            grad = grad + p.astype(f32)
        normalized = h.astype(f32) * scaled[:, None]
        hidden = scaled[:, None] * (grad * gain_block(0)[None, :] - normalized * row_dot[:, None])
        gain_grad = jnp.sum(grad * normalized, axis=0)
        gain_grad = gain_grad + dp_shift(gain_grad, 0, 0, 1)
        gain_grad = gain_grad + dp_shift(gain_grad, 0, 1, 0)
        gain_grad = gain_grad + sum(dp_shift(gain_grad, k, 0, 0) for k in range(1, na))
        return hidden, grad_head, gain_grad

    return shards


def solution(mesh):
    return jax.shard_map(
        make(mesh),
        mesh=mesh,
        in_specs=(P("dp", "tensor"), P(), P(None, "tensor"), P("dp")),
        out_specs=(P("dp", "tensor"), P("dp", "tensor"), P("tensor")),
        check_vma=False,
    )
```
